256 devices in a mesh: seq: 16 (over z, core), batch: 16 (over y, x).
Axes of the slice: x: 4, y: 4, z: 8, core: 2. Of those that a mesh axis runs over, the one named last changes fastest.
Arguments:
- features: bfloat16 [16, 2560, 1024], P('batch', 'seq'), may hold values from -6 to 6
- w_qk: bfloat16 [1024, 2048], replicated, may hold values from -0.1875 to 0.1875
- w_value: bfloat16 [1024, 1024], replicated, may hold values from -0.1875 to 0.1875
- w_gate: bfloat16 [1024, 1024], replicated, may hold values from -0.1875 to 0.1875
- cotangent: bfloat16 [16, 2560, 1024], P('batch', 'seq'), may hold values from -6 to 6
- lengths: int32 [16, 3], P('batch'), may hold values from 1 to 1280, 2560 in all within a row
Outputs:
- grad_qk_t: float32 [2048, 1024], P(('seq', 'batch'))
The draws below stay inside these ranges and needn't reach their ends.
Inputs may be any that keep to these rules, and one draw needn't show every extreme that they name: The 3 lengths of a group sum to 2560, and the longest is exactly 1280.
All inputs are finite; a program needn't handle non-finite values.
Results may differ from the reference program's by a relative error of at most 0.0053.
Values may be sent and summed in bfloat16 or wider, within the bound.
No kernel may reach another device: no remote copies, remote signals or barrier semaphores. Data moves between devices by JAX's collectives and lax.ppermute only.
A program may use at most 128 MiB of HBM per device.

```python
import math
import jax
import jax.numpy as jnp
import numpy as np
from jax import lax

D = 1024
HEADS = 8
USERS = 3
SEQ_LEN = 2560
N_BATCH = 16


def shard_levels(own_key, shape, shards, smallest, high):
    loudness, own = 1.0, jax.random.fold_in(own_key, 6)
    for position, blocks in shards:
        steps = jnp.exp(jax.random.uniform(jax.random.fold_in(own, position), (blocks,), jnp.float32, smallest / len(shards), high / len(shards)))
        loudness = loudness * jnp.repeat(steps, shape[position] // blocks).reshape([-1 if axis == position else 1 for axis in range(len(shape))])
    return loudness


def profile(count, total, limit, skew):
    weights = [(1 << 20) // math.isqrt(grade ** skew) + 1 for grade in range(2, count + 1)]
    rest, counts = total - limit - (count - 1), [1] * (count - 1)
    while rest > 0:
        movable = [i for i in range(count - 1) if counts[i] < limit]
        mass, remaining = sum([weights[i] for i in movable]), rest
        for i in movable:
            addition = min(limit - counts[i], max(1, remaining * weights[i] // mass), rest)
            counts[i] = counts[i] + addition
            rest = rest - addition
    return np.array([limit] + counts)


def ragged(rng, count, total, most, skew):
    if count == 2:
        one = jax.random.randint(rng, (), max(1, total - most), min(most, total - 1) + 1)
        return jnp.stack([one, total - one])
    tallies = jnp.asarray(profile(count, total, most, skew), jnp.int32)
    couples = (count - 1) // 2
    donor, sink = tallies[1:1 + 2 * couples:2], tallies[2:2 + 2 * couples:2]
    margin = jnp.minimum(donor - 1, most - sink)
    moved = jax.random.randint(jax.random.fold_in(rng, 1), (couples,), 0, 1 << 20) % (margin + 1)
    tallies = tallies.at[1:1 + 2 * couples:2].set(donor - moved).at[2:2 + 2 * couples:2].set(sink + moved)
    return tallies[jax.random.permutation(jax.random.fold_in(rng, 2), count)]


def normal_values(own_key, dims, scale, bound, shards=(), held_as=jnp.bfloat16):
    loudness = shard_levels(own_key, dims, shards, -0.22, 0.18) if shards else 1.0
    values = jax.random.normal(own_key, dims, jnp.float32) * scale * loudness
    return jnp.minimum(jnp.maximum(values, -bound), bound).astype(held_as)


def setup_inputs(seed: int = 0) -> dict:
    streams_of = jax.random.split(jax.random.key(seed), 7)
    return {
        "features": normal_values(streams_of[0], (N_BATCH, SEQ_LEN, D), 1.0, 6.0, ((0, 16), (1, 16))),
        "w_qk": normal_values(streams_of[1], (D, 2 * D), D ** -0.5, 0.1875),
        "w_value": normal_values(streams_of[2], (D, D), D ** -0.5, 0.1875),
        "w_gate": normal_values(streams_of[3], (D, D), D ** -0.5, 0.1875),
        "cotangent": normal_values(streams_of[4], (N_BATCH, SEQ_LEN, D), 1.0, 6.0, ((0, 16), (1, 16))),
        "lengths": jax.vmap(lambda own: ragged(own, USERS, SEQ_LEN, SEQ_LEN // 2, 2))(jax.random.split(streams_of[5], N_BATCH)).reshape((N_BATCH, USERS)).astype(jnp.int32),
    }


def silu_grad(z):
    s = jax.nn.sigmoid(z)
    return s * (1.0 + z * (1.0 - s))

def one_group(feats, cotan, lens, w_qk, w_value, w_gate):
    total = feats.shape[0]
    width = feats.shape[1]
    head_dim = width // HEADS
    scale_factor = head_dim ** (-0.5)
    ends = jnp.cumsum(lens).astype(jnp.int32)
    begins = (ends - lens).astype(jnp.int32)
    positions = jnp.arange(total, dtype=jnp.int32)
    inside = (positions[:, None] >= begins[None, :]) & (positions[:, None] < ends[None, :])
    user_begin = lax.optimization_barrier(jnp.sum(jnp.where(inside, begins[None, :], 0), axis=1)).astype(jnp.int32)
    mask = (positions[None, :] <= positions[:, None]) & (positions[None, :] >= user_begin[:, None])
    pre_qk = jnp.dot(feats, w_qk, preferred_element_type=jnp.float32)
    pre_v = jnp.dot(feats, w_value, preferred_element_type=jnp.float32)
    pre_u = jnp.dot(feats, w_gate, preferred_element_type=jnp.float32)
    query = jax.nn.silu(pre_qk[:, :width]).astype(jnp.bfloat16)
    key = jax.nn.silu(pre_qk[:, width:]).astype(jnp.bfloat16)
    value = jax.nn.silu(pre_v).astype(jnp.bfloat16)
    gate = jax.nn.silu(pre_u)
    q3 = query.astype(jnp.float32).reshape(total, HEADS, head_dim)
    k3 = key.astype(jnp.float32).reshape(total, HEADS, head_dim)
    v3 = value.astype(jnp.float32).reshape(total, HEADS, head_dim)
    scores = jnp.einsum('qhd,khd->hqk', q3, k3) * scale_factor
    weights = jnp.where(mask[None], jax.nn.silu(scores), 0.0).astype(jnp.bfloat16)
    attended = jnp.einsum('hqk,khd->qhd', weights.astype(jnp.float32), v3).reshape(total, width)
    mean = lax.optimization_barrier(jnp.mean(attended, axis=-1, keepdims=True))
    centered = attended - mean
    rstd = lax.rsqrt(lax.optimization_barrier(jnp.mean(centered * centered, axis=-1, keepdims=True)) + 1e-05)
    normed = centered * rstd
    grad_normed = cotan.astype(jnp.float32) * gate
    d_attended = rstd * (grad_normed - lax.optimization_barrier(jnp.mean(grad_normed, axis=-1, keepdims=True)) - normed * lax.optimization_barrier(jnp.mean(grad_normed * normed, axis=-1, keepdims=True)))
    d_attended = d_attended.astype(jnp.bfloat16)
    d3 = d_attended.astype(jnp.float32).reshape(total, HEADS, head_dim)
    d_weights = jnp.einsum('qhd,khd->hqk', d3, v3)
    d_scores = (jnp.where(mask[None], d_weights * silu_grad(scores), 0.0) * scale_factor).astype(jnp.bfloat16)
    d_scores32 = d_scores.astype(jnp.float32)
    d_query = jnp.einsum('hqk,khd->qhd', d_scores32, k3).reshape(total, width)
    d_key = jnp.einsum('hqk,qhd->khd', d_scores32, q3).reshape(total, width)
    d_pre = jnp.concatenate([d_query * silu_grad(pre_qk[:, :width]), d_key * silu_grad(pre_qk[:, width:])], axis=1).astype(jnp.bfloat16)
    return lax.dot_general(d_pre, feats, (((0,), (0,)), ((), ())), preferred_element_type=jnp.float32)

def reference(features, w_qk, w_value, w_gate, cotangent, lengths):
    width = features.shape[2]

    def step(carry, items):
        feats, cotan, lens = items
        return (carry + one_group(feats, cotan, lens, w_qk, w_value, w_gate), None)
    start = jnp.zeros((2 * width, width), jnp.float32)
    result, _ = lax.scan(step, start, (features, cotangent, lengths))
    return result
```

```python
import functools
import jax
import jax.numpy as jnp
from jax import lax
from jax.experimental import pallas as pl
from jax.experimental.pallas import tpu as pltpu
from jax.sharding import PartitionSpec as P

HEADS = 8
BLK = 256
F32 = jnp.float32
BF16 = jnp.bfloat16
VMEM_LIMIT = 56 * 1024 * 1024


def nn(a, b):
    return lax.dot_general(a, b, (((1,), (0,)), ((), ())), preferred_element_type=F32)


def nt(a, b):
    return lax.dot_general(a, b, (((1,), (1,)), ((), ())), preferred_element_type=F32)


def silu(z):
    half = 0.5 * z
    return half + half * jnp.tanh(half)


def silu_grad(z):
    half = 0.5 * z
    t = jnp.tanh(half)
    return 0.5 * (1.0 + t) * (1.0 + half * (1.0 - t))


def begin_of(pos, second, third):
    return jnp.where(pos >= third, third, jnp.where(pos >= second, second, 0))


def key_ranges(i, second, third):
    first = i * BLK
    low = begin_of(first, second, third) // BLK
    clear = (begin_of(first + BLK - 1, second, third) + BLK - 1) // BLK
    return low, jnp.minimum(jnp.maximum(clear, low), i)


def tile_mask(i, j, second, third):
    query = i * BLK + lax.broadcasted_iota(jnp.int32, (1, BLK), 1)
    begin = begin_of(query, second, third)
    key = j * BLK + lax.broadcasted_iota(jnp.int32, (BLK, BLK), 0)
    return (key <= query) & (key >= begin)


def forward_kernel(info, feats, wq, wk, wv, wu, cot, q_ref, k_ref, v_ref, qt_ref, kt_ref,
                   vt_ref, pre_ref, g_ref, att_ref, stat_ref, acc, *, scale):
    i = pl.program_id(0)
    role, second, third = info[1], info[2], info[3]
    rows = pl.ds(pl.multiple_of(i * BLK, BLK), BLK)
    x = feats[...]
    pre_q = nn(x, wq[...])
    pre_k = nn(x, wk[...])
    q = silu(pre_q).astype(BF16)
    k = silu(pre_k).astype(BF16)
    v = silu(nn(x, wv[...])).astype(BF16)
    gate = silu(nn(x, wu[...]))
    q_ref[rows, :] = q
    k_ref[rows, :] = k
    v_ref[rows, :] = v
    qt_ref[:, rows] = q.T
    kt_ref[:, rows] = k.T
    vt_ref[:, rows] = v.T
    pre_ref[:, rows] = jnp.where(role == 0, pre_q, pre_k).T
    g = (cot[...].astype(F32) * gate).T
    g_ref[:, rows] = g

    def tile(j, masked):
        keys = pl.ds(pl.multiple_of(j * BLK, BLK), BLK)
        half = nt(k_ref[keys, :], q) * (0.5 * scale)
        w = half + half * jnp.tanh(half)
        if masked:
            w = jnp.where(tile_mask(i, j, second, third), w, 0.0)
        acc[...] += nn(vt_ref[:, keys], w.astype(BF16))

    low, clear = key_ranges(i, second, third)
    acc[...] = jnp.zeros_like(acc)
    pl.loop(low, clear)(lambda j: tile(j, True))
    pl.loop(clear, i)(lambda j: tile(j, False))
    tile(i, True)
    att = acc[...]
    att_ref[:, rows] = att
    mean = jnp.mean(att, axis=0, keepdims=True)
    centered = att - mean
    stat_ref[0:1, rows] = mean
    stat_ref[1:2, rows] = jnp.sum(centered * centered, axis=0, keepdims=True)
    stat_ref[2:3, rows] = jnp.sum(g, axis=0, keepdims=True)
    stat_ref[3:4, rows] = jnp.sum(g * centered, axis=0, keepdims=True)


def backward_kernel(info, feats_hbm, q_ref, k_ref, v_ref, qt_ref, kt_ref, pre_ref, g_ref,
                    att_ref, stat_ref, out_ref, feats, datt, acc, sem, *, scale, width):
    role, second, third = info[1], info[2], info[3]
    total = q_ref.shape[0]
    blocks = total // BLK
    load = pltpu.make_async_copy(feats_hbm, feats, sem)
    load.start()
    mean = stat_ref[0:1, :]
    rstd = lax.rsqrt(stat_ref[1:2, :] / width + 1e-5)
    g_mean = stat_ref[2:3, :] / width
    gn_mean = stat_ref[3:4, :] * rstd / width
    normed = (att_ref[...] - mean) * rstd
    datt[...] = (rstd * (g_ref[...] - g_mean - normed * gn_mean)).astype(BF16)

    def d_scores(i, j, masked):
        queries = pl.ds(pl.multiple_of(i * BLK, BLK), BLK)
        keys = pl.ds(pl.multiple_of(j * BLK, BLK), BLK)
        half = nt(k_ref[keys, :], q_ref[queries, :]) * (0.5 * scale)
        dw = nn(v_ref[keys, :], datt[:, queries])
        t = jnp.tanh(half)
        ds = (1.0 + t) * (1.0 + half * (1.0 - t)) * dw
        if masked:
            ds = jnp.where(tile_mask(i, j, second, third), ds, 0.0)
        return ds.astype(BF16)

    acc[...] = jnp.zeros_like(acc)

    def query_tile(i, j, masked):
        queries = pl.ds(pl.multiple_of(i * BLK, BLK), BLK)
        keys = pl.ds(pl.multiple_of(j * BLK, BLK), BLK)
        acc[:, queries] += nn(kt_ref[:, keys], d_scores(i, j, masked))

    def key_tile(i, j, masked):
        queries = pl.ds(pl.multiple_of(i * BLK, BLK), BLK)
        keys = pl.ds(pl.multiple_of(j * BLK, BLK), BLK)
        acc[:, keys] += nt(qt_ref[:, queries], d_scores(i, j, masked))

    def sweep(tile):
        @pl.loop(0, blocks)
        def _(i):
            low, clear = key_ranges(i, second, third)
            pl.loop(low, clear)(lambda j: tile(i, j, True))
            pl.loop(clear, i)(lambda j: tile(i, j, False))
            tile(i, i, True)

    pl.when(role == 0)(lambda: sweep(query_tile))
    pl.when(role == 1)(lambda: sweep(key_tile))
    dpre = (acc[...] * (0.5 * scale) * silu_grad(pre_ref[...])).astype(BF16)
    load.wait()
    out_ref[...] = nn(dpre, feats[...]).astype(out_ref.dtype)


def body(features, w_qk, w_value, w_gate, cotangent, lengths):
    inputs = features[0]
    tok, width = inputs.shape
    n_seq = lax.axis_size("seq")
    n_batch = lax.axis_size("batch")
    total = tok * n_seq
    dim = width // HEADS
    scale = dim ** (-0.5)
    s = lax.axis_index("seq")
    head, role = s % HEADS, s // HEADS
    info = jnp.stack([head, role, lengths[0, 0], lengths[0, 0] + lengths[0, 1]]).astype(jnp.int32)
    feats = lax.all_gather(inputs, "seq", axis=0, tiled=True)
    pieces = jnp.moveaxis(cotangent[0].reshape(tok, HEADS, dim), 1, 0)
    pieces = jnp.concatenate([pieces, pieces], axis=0)
    cot = lax.all_to_all(pieces, "seq", 0, 0).reshape(total, dim)

    blocks = total // BLK
    whole = lambda shape: pl.BlockSpec(shape, lambda i, info: (0, 0))
    row = jax.ShapeDtypeStruct((total, dim), BF16)
    col = jax.ShapeDtypeStruct((dim, total), BF16)
    colf = jax.ShapeDtypeStruct((dim, total), F32)
    stat = jax.ShapeDtypeStruct((4, total), F32)
    q, k, v, qt, kt, vt, pre, g, att, stats = pl.pallas_call(
        functools.partial(forward_kernel, scale=scale),
        grid_spec=pltpu.PrefetchScalarGridSpec(
            num_scalar_prefetch=1,
            grid=(blocks,),
            in_specs=[
                pl.BlockSpec((BLK, width), lambda i, info: (i, 0)),
                pl.BlockSpec((width, dim), lambda i, info: (0, info[0])),
                pl.BlockSpec((width, dim), lambda i, info: (0, HEADS + info[0])),
                pl.BlockSpec((width, dim), lambda i, info: (0, info[0])),
                pl.BlockSpec((width, dim), lambda i, info: (0, info[0])),
                pl.BlockSpec((BLK, dim), lambda i, info: (i, 0)),
            ],
            out_specs=[whole(a.shape) for a in (row, row, row, col, col, col, colf, colf, colf, stat)],
            scratch_shapes=[pltpu.VMEM((dim, BLK), F32)],
        ),
        out_shape=[row, row, row, col, col, col, colf, colf, colf, stat],
        compiler_params=pltpu.CompilerParams(vmem_limit_bytes=VMEM_LIMIT),
        name="forward",
    )(info, feats, w_qk, w_qk, w_value, w_gate, cot)

    count = dim
    for step in (1, 2, 4):
        other = lax.ppermute(stats, "seq", [(a, a ^ step) for a in range(n_seq)])
        delta = stats[0] - other[0]
        stats = jnp.stack([
            0.5 * (stats[0] + other[0]),
            stats[1] + other[1] + delta * delta * (0.5 * count),
            stats[2] + other[2],
            stats[3] + other[3] + 0.5 * delta * (stats[2] - other[2]),
        ])
        count = 2 * count

    vmem = pl.BlockSpec(memory_space=pltpu.VMEM)
    part = pl.pallas_call(
        functools.partial(backward_kernel, scale=scale, width=width),
        in_specs=[pl.BlockSpec(memory_space=pltpu.SMEM), pl.BlockSpec(memory_space=pl.ANY)] + [vmem] * 9,
        out_specs=vmem,
        out_shape=jax.ShapeDtypeStruct((dim, width), BF16),
        scratch_shapes=[
            pltpu.VMEM((total, width), BF16),
            pltpu.VMEM((dim, total), BF16),
            pltpu.VMEM((dim, total), F32),
            pltpu.SemaphoreType.DMA,
        ],
        compiler_params=pltpu.CompilerParams(vmem_limit_bytes=VMEM_LIMIT),
        name="backward",
    )(info, feats, q, k, v, qt, kt, pre, g, att, stats)
    parts = lax.all_to_all(part.reshape(n_batch, dim // n_batch, width), "batch", 0, 0)
    return jnp.sum(parts.astype(F32), axis=0)


def solution(mesh):
    return jax.shard_map(
        body,
        mesh=mesh,
        in_specs=(
            P("batch", "seq", None),
            P(),
            P(),
            P(),
            P("batch", "seq", None),
            P("batch", None),
        ),
        out_specs=P(("seq", "batch"), None),
        check_vma=False,
    )
```

```python
import functools
import jax
import jax.numpy as jnp
from jax import lax
from jax.experimental import pallas as pl
from jax.experimental.pallas import tpu as pltpu
from jax.sharding import PartitionSpec as P

HEADS = 8
BLK = 256
UNROLL = 4
WIDE = 512
F32 = jnp.float32
BF16 = jnp.bfloat16
VMEM_LIMIT = 46 * 1024 * 1024


def nn(a, b):
    return lax.dot_general(a, b, (((1,), (0,)), ((), ())), preferred_element_type=F32)


def nt(a, b):
    return lax.dot_general(a, b, (((1,), (1,)), ((), ())), preferred_element_type=F32)


def silu(z):
    half = 0.5 * z
    return half + half * jnp.tanh(half)


def silu_grad(z):
    half = 0.5 * z
    t = jnp.tanh(half)
    return 0.5 * (1.0 + t) * (1.0 + half * (1.0 - t))


def begin_of(pos, second, third):
    return jnp.where(pos >= third, third, jnp.where(pos >= second, second, 0))


def plan_tiles(blocks, second, third):
    i = jnp.arange(blocks, dtype=jnp.int32)[:, None]
    j = jnp.arange(blocks, dtype=jnp.int32)[None, :]
    low = begin_of(i * BLK, second, third) // BLK
    clear = (begin_of(i * BLK + BLK - 1, second, third) + BLK - 1) // BLK
    used = (j >= low) & (j <= i)
    plain = (used & (j >= clear) & (j < i)).reshape(-1)
    edge = used.reshape(-1) & ~plain
    n_plain = jnp.sum(plain.astype(jnp.int32))
    n_all = n_plain + jnp.sum(edge.astype(jnp.int32))
    place = jnp.where(plain, jnp.cumsum(plain) - 1, jnp.where(edge, n_plain + jnp.cumsum(edge) - 1, -1))
    code = (i * blocks + j).reshape(-1)
    slot = jnp.arange(blocks * blocks + UNROLL, dtype=jnp.int32)
    table = jnp.sum(jnp.where(slot[:, None] == place[None, :], code[None, :], 0), axis=1)
    table = jnp.where(slot < n_all, table, blocks - 1)
    return table.astype(jnp.int32), n_plain, n_all


def block(index):
    return pl.ds(pl.multiple_of(index * BLK, BLK), BLK)


def tile_mask(i, j, second, third, query_rows):
    q_dim, shape = (0, (BLK, 128)) if query_rows else (1, (1, BLK))
    query = i * BLK + lax.broadcasted_iota(jnp.int32, shape, q_dim)
    begin = begin_of(query, second, third)
    if query_rows:
        parts = []
        for at in range(0, BLK, 128):
            key = j * BLK + at + lax.broadcasted_iota(jnp.int32, (BLK, 128), 1)
            parts.append((key <= query) & (key >= begin))
        return parts
    key = j * BLK + lax.broadcasted_iota(jnp.int32, (BLK, BLK), 0)
    return (key <= query) & (key >= begin)


def keep(values, mask):
    if isinstance(mask, list):
        cols = [jnp.where(m, values[:, n * 128:(n + 1) * 128], 0.0) for n, m in enumerate(mask)]
        return jnp.concatenate(cols, axis=1)
    return jnp.where(mask, values, 0.0)


def run_tiles(table, n_plain, n_all, blocks, begin_tile, end_tile):
    def entry(t):
        code = table[t]
        i = code // blocks
        return i, code - i * blocks

    def group(masked):
        def f(u, carry):
            tiles = [entry(u * UNROLL + n) for n in range(UNROLL)]
            state = begin_tile(*tiles[0])
            for n, tile in enumerate(tiles):
                following = begin_tile(*tiles[n + 1]) if n + 1 < UNROLL else None
                end_tile(*tile, state, masked)
                state = following
            return carry
        return f

    plain = n_plain // UNROLL
    lax.fori_loop(0, plain, group(False), 0)
    lax.fori_loop(plain, (n_all + UNROLL - 1) // UNROLL, group(True), 0)


def forward_kernel(info, table, feats_hbm, w_ref, cot, q_ref, k_ref, v_ref, pre_ref, g_ref,
                   att_ref, stat_ref, feats, acc, sem, *, scale):
    role, second, third = info[0], info[1], info[2]
    total, dim = q_ref.shape
    blocks = total // BLK
    loads = []
    for i in range(blocks):
        rows = pl.ds(i * BLK, BLK)
        loads.append(pltpu.make_async_copy(feats_hbm.at[rows, :], feats.at[rows, :], sem.at[i]))
        loads[-1].start()
    for i in range(total // WIDE):
        rows = pl.ds(i * WIDE, WIDE)
        for n in range(WIDE // BLK):
            loads[i * (WIDE // BLK) + n].wait()
        pre = nn(feats[rows, :], w_ref[...])
        pre_q, pre_k = pre[:, :dim], pre[:, dim:2 * dim]
        q_ref[rows, :] = silu(pre_q).astype(BF16)
        k_ref[rows, :] = silu(pre_k).astype(BF16)
        v_ref[rows, :] = silu(pre[:, 2 * dim:3 * dim]).astype(BF16)
        pre_ref[rows, :] = jnp.where(role == 0, pre_q, pre_k)
        g_ref[:, rows] = (cot[rows, :].astype(F32) * silu(pre[:, 3 * dim:])).T
    acc[...] = jnp.zeros_like(acc)

    def begin_tile(i, j):
        return nt(q_ref[block(i), :], k_ref[block(j), :])

    def end_tile(i, j, scores, masked):
        half = scores * (0.5 * scale)
        w = half + half * jnp.tanh(half)
        if masked:
            w = keep(w, tile_mask(i, j, second, third, True))
        acc[block(i), :] += nn(w.astype(BF16), v_ref[block(j), :])

    run_tiles(table, info[3], info[4], blocks, begin_tile, end_tile)
    for i in range(blocks):
        rows = pl.ds(i * BLK, BLK)
        att = acc[rows, :].T
        g = g_ref[:, rows]
        att_ref[:, rows] = att
        mean = jnp.mean(att, axis=0, keepdims=True)
        centered = att - mean
        stat_ref[0:1, rows] = mean
        stat_ref[1:2, rows] = jnp.sum(centered * centered, axis=0, keepdims=True)
        stat_ref[2:3, rows] = jnp.sum(g, axis=0, keepdims=True)
        stat_ref[3:4, rows] = jnp.sum(g * centered, axis=0, keepdims=True)


def backward_kernel(info, table, feats_hbm, q_ref, k_ref, v_ref, pre_ref, g_ref, att_ref,
                    stat_ref, out_ref, feats, datt, acc, dpre, sem, *, scale, width):
    role, second, third = info[0], info[1], info[2]
    total = q_ref.shape[0]
    blocks = total // BLK
    load = pltpu.make_async_copy(feats_hbm, feats, sem)
    load.start()
    for i in range(blocks):
        rows = pl.ds(i * BLK, BLK)
        mean = stat_ref[0:1, rows]
        rstd = lax.rsqrt(stat_ref[1:2, rows] / width + 1e-5)
        g_mean = stat_ref[2:3, rows] / width
        gn_mean = stat_ref[3:4, rows] * rstd / width
        normed = (att_ref[:, rows] - mean) * rstd
        d = rstd * (g_ref[:, rows] - g_mean - normed * gn_mean)
        datt[rows, :] = d.T.astype(BF16)
    acc[...] = jnp.zeros_like(acc)

    def d_scores(scores, dw, mask):
        half = scores * (0.5 * scale)
        t = jnp.tanh(half)
        ds = ((0.5 * scale) + (0.5 * scale) * t) * (1.0 + half * (1.0 - t)) * dw
        if mask is not None:
            ds = keep(ds, mask)
        return ds.astype(BF16)

    def query_begin(i, j):
        return (nt(q_ref[block(i), :], k_ref[block(j), :]), nt(datt[block(i), :], v_ref[block(j), :]))

    def query_end(i, j, state, masked):
        ds = d_scores(*state, tile_mask(i, j, second, third, True) if masked else None)
        acc[block(i), :] += nn(ds, k_ref[block(j), :])

    def key_begin(i, j):
        return (nt(k_ref[block(j), :], q_ref[block(i), :]), nt(v_ref[block(j), :], datt[block(i), :]))

    def key_end(i, j, state, masked):
        ds = d_scores(*state, tile_mask(i, j, second, third, False) if masked else None)
        acc[block(j), :] += nn(ds, q_ref[block(i), :])

    pl.when(role == 0)(lambda: run_tiles(table, info[3], info[4], blocks, query_begin, query_end))
    pl.when(role == 1)(lambda: run_tiles(table, info[3], info[4], blocks, key_begin, key_end))
    for i in range(blocks):
        rows = pl.ds(i * BLK, BLK)
        dpre[:, rows] = (acc[rows, :] * silu_grad(pre_ref[rows, :])).T.astype(BF16)
    load.wait()
    out_ref[...] = nn(dpre[...], feats[...]).astype(out_ref.dtype)


def body(features, w_qk, w_value, w_gate, cotangent, lengths):
    inputs = features[0]
    tok, width = inputs.shape
    n_seq = lax.axis_size("seq")
    n_batch = lax.axis_size("batch")
    total = tok * n_seq
    dim = width // HEADS
    scale = dim ** (-0.5)
    blocks = total // BLK
    s = lax.axis_index("seq")
    head, role = s % HEADS, s // HEADS
    feats = lax.all_gather(inputs, "seq", axis=0, tiled=True)
    pieces = jnp.moveaxis(cotangent[0].reshape(tok, HEADS, dim), 1, 0)
    pieces = jnp.concatenate([pieces, pieces], axis=0)
    cot = lax.all_to_all(pieces, "seq", 0, 0).reshape(total, dim)
    second = lengths[0, 0]
    third = second + lengths[0, 1]
    table, n_plain, n_all = plan_tiles(blocks, second, third)
    info = jnp.stack([role, second, third, n_plain, n_all]).astype(jnp.int32)
    columns = lambda w, at: lax.dynamic_slice_in_dim(w, at * dim, dim, 1)
    weights = jnp.concatenate([
        columns(w_qk, head), columns(w_qk, HEADS + head), columns(w_value, head), columns(w_gate, head),
    ], axis=1)

    smem = pl.BlockSpec(memory_space=pltpu.SMEM)
    vmem = pl.BlockSpec(memory_space=pltpu.VMEM)
    hbm = pl.BlockSpec(memory_space=pltpu.HBM)
    row = jax.ShapeDtypeStruct((total, dim), BF16)
    rowf = jax.ShapeDtypeStruct((total, dim), F32)
    colf = jax.ShapeDtypeStruct((dim, total), F32)
    stat = jax.ShapeDtypeStruct((4, total), F32)
    q, k, v, pre, g, att, stats = pl.pallas_call(
        functools.partial(forward_kernel, scale=scale),
        in_specs=[smem, smem, hbm, vmem, vmem],
        out_specs=[vmem] * 7,
        out_shape=[row, row, row, rowf, colf, colf, stat],
        scratch_shapes=[
            pltpu.VMEM((total, width), BF16),
            pltpu.VMEM((total, dim), F32),
            pltpu.SemaphoreType.DMA((blocks,)),
        ],
        compiler_params=pltpu.CompilerParams(vmem_limit_bytes=VMEM_LIMIT),
        name="forward",
    )(info, table, feats, weights, cot)

    count = dim
    for step in (1, 2, 4):
        other = lax.ppermute(stats, "seq", [(a, a ^ step) for a in range(n_seq)])
        delta = stats[0] - other[0]
        stats = jnp.stack([
            0.5 * (stats[0] + other[0]),
            stats[1] + other[1] + delta * delta * (0.5 * count),
            stats[2] + other[2],
            stats[3] + other[3] + 0.5 * delta * (stats[2] - other[2]),
        ])
        count = 2 * count

    part = pl.pallas_call(
        functools.partial(backward_kernel, scale=scale, width=width),
        in_specs=[smem, smem, hbm] + [vmem] * 7,
        out_specs=vmem,
        out_shape=jax.ShapeDtypeStruct((dim, width), BF16),
        scratch_shapes=[
            pltpu.VMEM((total, width), BF16),
            pltpu.VMEM((total, dim), BF16),
            pltpu.VMEM((total, dim), F32),
            pltpu.VMEM((dim, total), BF16),
            pltpu.SemaphoreType.DMA,
        ],
        compiler_params=pltpu.CompilerParams(vmem_limit_bytes=VMEM_LIMIT),
        name="backward",
    )(info, table, feats, q, k, v, pre, g, att, stats)
    parts = lax.all_to_all(part.reshape(n_batch, dim // n_batch, width), "batch", 0, 0)
    return jnp.sum(parts.astype(F32), axis=0)


def solution(mesh):
    return jax.shard_map(
        body,
        mesh=mesh,
        in_specs=(
            P("batch", "seq", None),
            P(),
            P(),
            P(),
            P("batch", "seq", None),
            P("batch", None),
        ),
        out_specs=P(("seq", "batch"), None),
        check_vma=False,
    )
```

```python
import functools
import jax
import jax.numpy as jnp
from jax import lax
from jax.experimental import pallas as pl
from jax.experimental.pallas import tpu as pltpu
from jax.sharding import PartitionSpec as P

HEADS = 8
BLK = 256
UNROLL = 4
WIDE = 512
F32 = jnp.float32
BF16 = jnp.bfloat16
ROLE, SECOND, THIRD, PLAIN, ALL, CHIP, CORE, TABLE = range(8)
VMEM_LIMIT = 46 * 1024 * 1024


def nn(a, b):
    return lax.dot_general(a, b, (((1,), (0,)), ((), ())), preferred_element_type=F32)


def nt(a, b):
    return lax.dot_general(a, b, (((1,), (1,)), ((), ())), preferred_element_type=F32)


def silu(z):
    half = 0.5 * z
    return half + half * jnp.tanh(half)


def silu_grad(z):
    half = 0.5 * z
    t = jnp.tanh(half)
    return 0.5 * (1.0 + t) * (1.0 + half * (1.0 - t))


def begin_of(pos, second, third):
    return jnp.where(pos >= third, third, jnp.where(pos >= second, second, 0))


def write_plan(plan, lengths, blocks):
    s = lax.axis_index("seq")
    second = lengths[0, 0]
    third = second + lengths[0, 1]
    plan[ROLE] = lax.div(s, HEADS)
    plan[SECOND] = second
    plan[THIRD] = third
    plan[CHIP] = lax.div(s, 2)
    plan[CORE] = lax.rem(s, 2)

    def emit(i, low, high, n):
        def put(j, at):
            plan[TABLE + at] = i * blocks + j
            return at + 1
        return lax.fori_loop(low, high, put, n)

    ranges = []
    for i in range(blocks):
        low = lax.div(begin_of(i * BLK, second, third), BLK)
        clear = lax.div(begin_of(i * BLK + BLK - 1, second, third) + BLK - 1, BLK)
        ranges.append((low, jnp.minimum(jnp.maximum(clear, low), i)))
    n = jnp.int32(0)
    for i, (low, clear) in enumerate(ranges):
        n = emit(i, clear, i, n)
    plan[PLAIN] = n
    for i, (low, clear) in enumerate(ranges):
        n = emit(i, low, clear, n)
        plan[TABLE + n] = i * blocks + i
        n = n + 1
    plan[ALL] = n
    for pad in range(UNROLL):
        plan[TABLE + n + pad] = blocks - 1


def block(index):
    return pl.ds(pl.multiple_of(index * BLK, BLK), BLK)


def tile_mask(i, j, second, third, query_rows):
    q_dim, shape = (0, (BLK, 128)) if query_rows else (1, (1, BLK))
    query = i * BLK + lax.broadcasted_iota(jnp.int32, shape, q_dim)
    begin = begin_of(query, second, third)
    if query_rows:
        parts = []
        for at in range(0, BLK, 128):
            key = j * BLK + at + lax.broadcasted_iota(jnp.int32, (BLK, 128), 1)
            parts.append((key <= query) & (key >= begin))
        return parts
    key = j * BLK + lax.broadcasted_iota(jnp.int32, (BLK, BLK), 0)
    return (key <= query) & (key >= begin)


def keep(values, mask):
    if isinstance(mask, list):
        cols = [jnp.where(m, values[:, n * 128:(n + 1) * 128], 0.0) for n, m in enumerate(mask)]
        return jnp.concatenate(cols, axis=1)
    return jnp.where(mask, values, 0.0)


def run_tiles(table, n_plain, n_all, blocks, begin_tile, end_tile):
    def entry(t):
        code = table[TABLE + t]
        i = code // blocks
        return i, code - i * blocks

    def group(masked):
        def f(u, carry):
            tiles = [entry(u * UNROLL + n) for n in range(UNROLL)]
            state = begin_tile(*tiles[0])
            for n, tile in enumerate(tiles):
                following = begin_tile(*tiles[n + 1]) if n + 1 < UNROLL else None
                end_tile(*tile, state, masked)
                state = following
            return carry
        return f

    plain = n_plain // UNROLL
    lax.fori_loop(0, plain, group(False), 0)
    lax.fori_loop(plain, (n_all + UNROLL - 1) // UNROLL, group(True), 0)


def prepare_kernel(lengths, own, wqk_hbm, wv_hbm, wu_hbm, plan, w_ref, feats, sem, own_sem, *, blocks):
    s = lax.axis_index("seq")
    dim = w_ref.shape[1] // 4
    head = lax.rem(s, HEADS) * dim
    width = wv_hbm.shape[1]
    tok = own.shape[0]
    copies = [pltpu.make_async_copy(own, feats.at[pl.ds(pl.multiple_of(s * tok, 16), tok), :], own_sem)]
    for n, (source, at) in enumerate(((wqk_hbm, head), (wqk_hbm, width + head), (wv_hbm, head), (wu_hbm, head))):
        columns = pl.ds(pl.multiple_of(at, 128), dim)
        copies.append(pltpu.make_async_copy(
            source.at[:, columns], w_ref.at[:, pl.ds(n * dim, dim)], sem.at[n]))
    for copy in copies:
        copy.start()
    write_plan(plan, lengths, blocks)
    for copy in copies:
        copy.wait()


def forward_kernel(plan, w_ref, cot, feats_hbm, q_ref, k_ref, v_ref, pre_ref, g_ref, att_ref,
                   stat_ref, feats, acc, sem, *, scale):
    role, second, third = plan[ROLE], plan[SECOND], plan[THIRD]
    total, dim = q_ref.shape
    blocks = total // BLK
    loads = []
    for i in range(total // WIDE):
        rows = pl.ds(i * WIDE, WIDE)
        loads.append(pltpu.make_async_copy(feats_hbm.at[rows, :], feats.at[rows, :], sem.at[i]))
        loads[-1].start()
    acc[...] = jnp.zeros_like(acc)
    for i in range(total // WIDE):
        rows = pl.ds(i * WIDE, WIDE)
        loads[i].wait()
        pre = nn(feats[rows, :], w_ref[...])
        pre_q, pre_k = pre[:, :dim], pre[:, dim:2 * dim]
        q_ref[rows, :] = silu(pre_q).astype(BF16)
        k_ref[rows, :] = silu(pre_k).astype(BF16)
        v_ref[rows, :] = silu(pre[:, 2 * dim:3 * dim]).astype(BF16)
        pre_ref[rows, :] = jnp.where(role == 0, pre_q, pre_k)
        g_ref[:, rows] = (cot[rows, :].astype(F32) * silu(pre[:, 3 * dim:])).T

    def begin_tile(i, j):
        return nt(q_ref[block(i), :], k_ref[block(j), :])

    def end_tile(i, j, scores, masked):
        half = scores * (0.5 * scale)
        w = half + half * jnp.tanh(half)
        if masked:
            w = keep(w, tile_mask(i, j, second, third, True))
        acc[block(i), :] += nn(w.astype(BF16), v_ref[block(j), :])

    run_tiles(plan, plan[PLAIN], plan[ALL], blocks, begin_tile, end_tile)
    for i in range(blocks):
        rows = pl.ds(i * BLK, BLK)
        att = acc[rows, :].T
        g = g_ref[:, rows]
        att_ref[:, rows] = att
        mean = jnp.mean(att, axis=0, keepdims=True)
        centered = att - mean
        stat_ref[0:1, rows] = mean
        stat_ref[1:2, rows] = jnp.sum(centered * centered, axis=0, keepdims=True)
        stat_ref[2:3, rows] = jnp.sum(g, axis=0, keepdims=True)
        stat_ref[3:4, rows] = jnp.sum(g * centered, axis=0, keepdims=True)


def backward_kernel(plan, feats_hbm, q_ref, k_ref, v_ref, pre_ref, g_ref, att_ref, stat_ref,
                    out_ref, feats, datt, acc, dpre, sem, *, scale, width):
    table = plan
    role, second, third = plan[ROLE], plan[SECOND], plan[THIRD]
    total = q_ref.shape[0]
    blocks = total // BLK
    load = pltpu.make_async_copy(feats_hbm, feats, sem)
    load.start()
    for i in range(blocks):
        rows = pl.ds(i * BLK, BLK)
        mean = stat_ref[0:1, rows]
        rstd = lax.rsqrt(stat_ref[1:2, rows] / width + 1e-5)
        g_mean = stat_ref[2:3, rows] / width
        gn_mean = stat_ref[3:4, rows] * rstd / width
        normed = (att_ref[:, rows] - mean) * rstd
        d = rstd * (g_ref[:, rows] - g_mean - normed * gn_mean)
        datt[rows, :] = d.T.astype(BF16)
    acc[...] = jnp.zeros_like(acc)

    def d_scores(scores, dw, mask):
        half = scores * (0.5 * scale)
        t = jnp.tanh(half)
        ds = ((0.5 * scale) + (0.5 * scale) * t) * (1.0 + half * (1.0 - t)) * dw
        if mask is not None:
            ds = keep(ds, mask)
        return ds.astype(BF16)

    def query_begin(i, j):
        return (nt(q_ref[block(i), :], k_ref[block(j), :]), nt(datt[block(i), :], v_ref[block(j), :]))

    def query_end(i, j, state, masked):
        ds = d_scores(*state, tile_mask(i, j, second, third, True) if masked else None)
        acc[block(i), :] += nn(ds, k_ref[block(j), :])

    def key_begin(i, j):
        return (nt(k_ref[block(j), :], q_ref[block(i), :]), nt(v_ref[block(j), :], datt[block(i), :]))

    def key_end(i, j, state, masked):
        ds = d_scores(*state, tile_mask(i, j, second, third, False) if masked else None)
        acc[block(j), :] += nn(ds, q_ref[block(i), :])

    pl.when(role == 0)(lambda: run_tiles(table, plan[PLAIN], plan[ALL], blocks, query_begin, query_end))
    pl.when(role == 1)(lambda: run_tiles(table, plan[PLAIN], plan[ALL], blocks, key_begin, key_end))
    for i in range(blocks):
        rows = pl.ds(i * BLK, BLK)
        dpre[:, rows] = (acc[rows, :] * silu_grad(pre_ref[rows, :])).T.astype(BF16)
    load.wait()
    out_ref[...] = nn(dpre[...], feats[...]).astype(out_ref.dtype)


def body(features, w_qk, w_value, w_gate, cotangent, lengths):
    inputs = features[0]
    tok, width = inputs.shape
    n_seq = lax.axis_size("seq")
    n_batch = lax.axis_size("batch")
    total = tok * n_seq
    dim = width // HEADS
    scale = dim ** (-0.5)
    blocks = total // BLK
    chips = n_seq // 2
    half = tok // 2
    s = lax.axis_index("seq")
    core = s % 2

    def shift(x, by):
        return lax.ppermute(x, "seq", [(a, (a + 2 * by) % n_seq) for a in range(n_seq)])

    def swap(x):
        return lax.ppermute(x, "seq", [(a, a ^ 1) for a in range(n_seq)])

    def place(feats, piece, by, other, offset=0):
        first = ((s // 2 + by) % chips * 2 + (1 - core if other else core)) * tok + offset
        return lax.dynamic_update_slice(feats, piece, (first, 0))

    smem = pl.BlockSpec(memory_space=pltpu.SMEM)
    vmem = pl.BlockSpec(memory_space=pltpu.VMEM)
    hbm = pl.BlockSpec(memory_space=pltpu.HBM)
    params = pltpu.CompilerParams(vmem_limit_bytes=VMEM_LIMIT)

    plan, weights, feats = pl.pallas_call(
        functools.partial(prepare_kernel, blocks=blocks),
        in_specs=[smem] + [hbm] * 4,
        out_specs=[smem, vmem, hbm],
        out_shape=[
            jax.ShapeDtypeStruct((TABLE + blocks * blocks + UNROLL,), jnp.int32),
            jax.ShapeDtypeStruct((width, 4 * dim), BF16),
            jax.ShapeDtypeStruct((total, width), BF16),
        ],
        scratch_shapes=[pltpu.SemaphoreType.DMA((4,)), pltpu.SemaphoreType.DMA],
        compiler_params=params,
        cost_estimate=pl.CostEstimate(flops=0, bytes_accessed=8 * 10 ** 6, transcendentals=0),
        name="prepare",
    )(lengths, inputs, w_qk, w_value, w_gate)

    cots = jnp.moveaxis(cotangent[0].reshape(tok, HEADS, dim), 1, 0)
    cots = jnp.concatenate([cots, cots], axis=0)
    feats = place(feats, swap(inputs), 0, True)
    right = left = inputs
    for step in range(1, chips // 2 + 1):
        last = step == chips // 2
        right = shift(right[:half] if last else right, 1)
        if step > 1:
            left, feats = lax.optimization_barrier((left, feats))
        left = shift(left[half:] if last else left, -1)
        if step == 2:
            cots, right, left = lax.optimization_barrier((cots, right, left))
        if step > 1:
            for piece in pending:
                feats = place(feats, *piece)
        if last:
            right, left, feats = lax.optimization_barrier((right, left, feats))
            for other in (False, True):
                feats = place(feats, swap(right) if other else right, step, other)
                feats = place(feats, swap(left) if other else left, step, other, half)
        else:
            pending = [(right, -step, False), (left, step, False), (swap(right), -step, True), (swap(left), step, True)]
    cot = lax.all_to_all(cots, "seq", 0, 0).reshape(total, dim)

    row = jax.ShapeDtypeStruct((total, dim), BF16)
    rowf = jax.ShapeDtypeStruct((total, dim), F32)
    colf = jax.ShapeDtypeStruct((dim, total), F32)
    stat = jax.ShapeDtypeStruct((4, total), F32)
    q, k, v, pre, g, att, stats = pl.pallas_call(
        functools.partial(forward_kernel, scale=scale),
        in_specs=[smem, vmem, vmem, hbm],
        out_specs=[vmem] * 7,
        out_shape=[row, row, row, rowf, colf, colf, stat],
        scratch_shapes=[
            pltpu.VMEM((total, width), BF16),
            pltpu.VMEM((total, dim), F32),
            pltpu.SemaphoreType.DMA((total // WIDE,)),
        ],
        compiler_params=params,
        cost_estimate=pl.CostEstimate(flops=12 * 10 ** 9, bytes_accessed=12 * 10 ** 6, transcendentals=0),
        name="forward",
    )(plan, weights, cot, feats)

    count = dim
    for step in (1, 2, 4):
        other = lax.ppermute(stats, "seq", [(a, a ^ step) for a in range(n_seq)])
        delta = stats[0] - other[0]
        stats = jnp.stack([
            0.5 * (stats[0] + other[0]),
            stats[1] + other[1] + delta * delta * (0.5 * count),
            stats[2] + other[2],
            stats[3] + other[3] + 0.5 * delta * (stats[2] - other[2]),
        ])
        count = 2 * count

    part = pl.pallas_call(
        functools.partial(backward_kernel, scale=scale, width=width),
        in_specs=[smem, hbm] + [vmem] * 7,
        out_specs=vmem,
        out_shape=jax.ShapeDtypeStruct((dim, width), BF16),
        scratch_shapes=[
            pltpu.VMEM((total, width), BF16),
            pltpu.VMEM((total, dim), BF16),
            pltpu.VMEM((total, dim), F32),
            pltpu.VMEM((dim, total), BF16),
            pltpu.SemaphoreType.DMA,
        ],
        compiler_params=params,
        name="backward",
    )(plan, feats, q, k, v, pre, g, att, stats)
    parts = lax.all_to_all(part.reshape(n_batch, dim // n_batch, width), "batch", 0, 0)
    return jnp.sum(parts.astype(F32), axis=0)


def solution(mesh):
    return jax.shard_map(
        body,
        mesh=mesh,
        in_specs=(
            P("batch", "seq", None),
            P(),
            P(),
            P(),
            P("batch", "seq", None),
            P("batch", None),
        ),
        out_specs=P(("seq", "batch"), None),
        check_vma=False,
    )
```

```python
import functools
import jax
import jax.numpy as jnp
from jax import lax
from jax.experimental import pallas as pl
from jax.experimental.pallas import tpu as pltpu
from jax.sharding import PartitionSpec as P

HEADS = 8
BLK = 256
UNROLL = 4
WIDE = 512
F32 = jnp.float32
BF16 = jnp.bfloat16
ROLE, SECOND, THIRD, PLAIN, ALL, CHIP, CORE, TABLE = range(8)
VMEM_LIMIT = 46 * 1024 * 1024


def nn(a, b):
    return lax.dot_general(a, b, (((1,), (0,)), ((), ())), preferred_element_type=F32)


def nt(a, b):
    return lax.dot_general(a, b, (((1,), (1,)), ((), ())), preferred_element_type=F32)


def silu(z):
    half = 0.5 * z
    return half + half * jnp.tanh(half)


def silu_grad(z):
    half = 0.5 * z
    t = jnp.tanh(half)
    return 0.5 * (1.0 + t) * (1.0 + half * (1.0 - t))


def begin_of(pos, second, third):
    return jnp.where(pos >= third, third, jnp.where(pos >= second, second, 0))


def write_plan(plan, lengths, blocks):
    s = lax.axis_index("seq")
    second = lengths[0, 0]
    third = second + lengths[0, 1]
    plan[ROLE] = lax.div(s, HEADS)
    plan[SECOND] = second
    plan[THIRD] = third
    plan[CHIP] = lax.div(s, 2)
    plan[CORE] = lax.rem(s, 2)

    def emit(i, low, high, n):
        def put(j, at):
            plan[TABLE + at] = i * blocks + j
            return at + 1
        return lax.fori_loop(low, high, put, n)

    ranges = []
    for i in range(blocks):
        low = lax.div(begin_of(i * BLK, second, third), BLK)
        clear = lax.div(begin_of(i * BLK + BLK - 1, second, third) + BLK - 1, BLK)
        ranges.append((low, jnp.minimum(jnp.maximum(clear, low), i)))
    n = jnp.int32(0)
    for i, (low, clear) in enumerate(ranges):
        n = emit(i, clear, i, n)
    plan[PLAIN] = n
    for i, (low, clear) in enumerate(ranges):
        n = emit(i, low, clear, n)
        plan[TABLE + n] = i * blocks + i
        n = n + 1
    plan[ALL] = n
    for pad in range(UNROLL):
        plan[TABLE + n + pad] = blocks - 1


def block(index):
    return pl.ds(pl.multiple_of(index * BLK, BLK), BLK)


def tile_mask(i, j, second, third, query_rows):
    q_dim, shape = (0, (BLK, 128)) if query_rows else (1, (1, BLK))
    query = i * BLK + lax.broadcasted_iota(jnp.int32, shape, q_dim)
    begin = begin_of(query, second, third)
    if query_rows:
        parts = []
        for at in range(0, BLK, 128):
            key = j * BLK + at + lax.broadcasted_iota(jnp.int32, (BLK, 128), 1)
            parts.append((key <= query) & (key >= begin))
        return parts
    key = j * BLK + lax.broadcasted_iota(jnp.int32, (BLK, BLK), 0)
    return (key <= query) & (key >= begin)


def keep(values, mask):
    if isinstance(mask, list):
        cols = [jnp.where(m, values[:, n * 128:(n + 1) * 128], 0.0) for n, m in enumerate(mask)]
        return jnp.concatenate(cols, axis=1)
    return jnp.where(mask, values, 0.0)


def run_tiles(table, n_plain, n_all, blocks, begin_tile, end_tile):
    def entry(t):
        code = table[TABLE + t]
        i = code // blocks
        return i, code - i * blocks

    def group(masked):
        def f(u, carry):
            tiles = [entry(u * UNROLL + n) for n in range(UNROLL)]
            state = begin_tile(*tiles[0])
            for n, tile in enumerate(tiles):
                following = begin_tile(*tiles[n + 1]) if n + 1 < UNROLL else None
                end_tile(*tile, state, masked)
                state = following
            return carry
        return f

    plain = n_plain // UNROLL
    lax.fori_loop(0, plain, group(False), 0)
    lax.fori_loop(plain, (n_all + UNROLL - 1) // UNROLL, group(True), 0)


def prepare_kernel(lengths, own, wqk_hbm, wv_hbm, wu_hbm, plan, w_ref, feats, sem, own_sem, *, blocks):
    s = lax.axis_index("seq")
    dim = w_ref.shape[1] // 4
    head = lax.rem(s, HEADS) * dim
    width = wv_hbm.shape[1]
    tok = own.shape[0]
    copies = [pltpu.make_async_copy(own, feats.at[pl.ds(pl.multiple_of(s * tok, 16), tok), :], own_sem)]
    for n, (source, at) in enumerate(((wqk_hbm, head), (wqk_hbm, width + head), (wv_hbm, head), (wu_hbm, head))):
        columns = pl.ds(pl.multiple_of(at, 128), dim)
        copies.append(pltpu.make_async_copy(
            source.at[:, columns], w_ref.at[:, pl.ds(n * dim, dim)], sem.at[n]))
    for copy in copies:
        copy.start()
    write_plan(plan, lengths, blocks)
    for copy in copies:
        copy.wait()


def forward_kernel(plan, w_ref, cot, feats_hbm, q_ref, k_ref, v_ref, pre_ref, g_ref, att_ref,
                   stat_ref, feats, acc, sem, *, scale):
    role, second, third = plan[ROLE], plan[SECOND], plan[THIRD]
    total, dim = q_ref.shape
    blocks = total // BLK
    loads = []
    for i in range(total // WIDE):
        rows = pl.ds(i * WIDE, WIDE)
        loads.append(pltpu.make_async_copy(feats_hbm.at[rows, :], feats.at[rows, :], sem.at[i]))
        loads[-1].start()
    acc[...] = jnp.zeros_like(acc)
    for i in range(total // WIDE):
        rows = pl.ds(i * WIDE, WIDE)
        loads[i].wait()
        pre = nn(feats[rows, :], w_ref[...])
        pre_q, pre_k = pre[:, :dim], pre[:, dim:2 * dim]
        q_ref[rows, :] = silu(pre_q).astype(BF16)
        k_ref[rows, :] = silu(pre_k).astype(BF16)
        v_ref[rows, :] = silu(pre[:, 2 * dim:3 * dim]).astype(BF16)
        pre_ref[rows, :] = jnp.where(role == 0, pre_q, pre_k)
        g_ref[:, rows] = (cot[rows, :].astype(F32) * silu(pre[:, 3 * dim:])).T

    def begin_tile(i, j):
        return nt(q_ref[block(i), :], k_ref[block(j), :])

    def end_tile(i, j, scores, masked):
        half = scores * (0.5 * scale)
        w = half + half * jnp.tanh(half)
        if masked:
            w = keep(w, tile_mask(i, j, second, third, True))
        acc[block(i), :] += nn(w.astype(BF16), v_ref[block(j), :])

    run_tiles(plan, plan[PLAIN], plan[ALL], blocks, begin_tile, end_tile)
    for i in range(blocks):
        rows = pl.ds(i * BLK, BLK)
        att = acc[rows, :].T
        g = g_ref[:, rows]
        att_ref[:, rows] = att
        mean = jnp.mean(att, axis=0, keepdims=True)
        centered = att - mean
        stat_ref[0:1, rows] = mean
        stat_ref[1:2, rows] = jnp.sum(centered * centered, axis=0, keepdims=True)
        stat_ref[2:3, rows] = jnp.sum(g, axis=0, keepdims=True)
        stat_ref[3:4, rows] = jnp.sum(g * centered, axis=0, keepdims=True)


def backward_kernel(plan, feats_hbm, q_ref, k_ref, v_ref, pre_ref, g_ref, att_ref, stat_ref,
                    out_ref, feats, datt, acc, dpre, sem, *, scale, width):
    table = plan
    role, second, third = plan[ROLE], plan[SECOND], plan[THIRD]
    total = q_ref.shape[0]
    blocks = total // BLK
    load = pltpu.make_async_copy(feats_hbm, feats, sem)
    load.start()
    for i in range(blocks):
        rows = pl.ds(i * BLK, BLK)
        mean = stat_ref[0:1, rows]
        rstd = lax.rsqrt(stat_ref[1:2, rows] / width + 1e-5)
        g_mean = stat_ref[2:3, rows] / width
        gn_mean = stat_ref[3:4, rows] * rstd / width
        normed = (att_ref[:, rows] - mean) * rstd
        d = rstd * (g_ref[:, rows] - g_mean - normed * gn_mean)
        datt[rows, :] = d.T.astype(BF16)
    acc[...] = jnp.zeros_like(acc)

    def d_scores(scores, dw, mask):
        half = scores * (0.5 * scale)
        t = jnp.tanh(half)
        ds = ((0.5 * scale) + (0.5 * scale) * t) * (1.0 + half * (1.0 - t)) * dw
        if mask is not None:
            ds = keep(ds, mask)
        return ds.astype(BF16)

    def query_begin(i, j):
        return (nt(q_ref[block(i), :], k_ref[block(j), :]), nt(datt[block(i), :], v_ref[block(j), :]))

    def query_end(i, j, state, masked):
        ds = d_scores(*state, tile_mask(i, j, second, third, True) if masked else None)
        acc[block(i), :] += nn(ds, k_ref[block(j), :])

    def key_begin(i, j):
        return (nt(k_ref[block(j), :], q_ref[block(i), :]), nt(v_ref[block(j), :], datt[block(i), :]))

    def key_end(i, j, state, masked):
        ds = d_scores(*state, tile_mask(i, j, second, third, False) if masked else None)
        acc[block(j), :] += nn(ds, q_ref[block(i), :])

    pl.when(role == 0)(lambda: run_tiles(table, plan[PLAIN], plan[ALL], blocks, query_begin, query_end))
    pl.when(role == 1)(lambda: run_tiles(table, plan[PLAIN], plan[ALL], blocks, key_begin, key_end))
    for i in range(blocks):
        rows = pl.ds(i * BLK, BLK)
        dpre[:, rows] = (acc[rows, :] * silu_grad(pre_ref[rows, :])).T.astype(BF16)
    load.wait()
    out_ref[...] = nn(dpre[...], feats[...]).astype(out_ref.dtype)


def body(features, w_qk, w_value, w_gate, cotangent, lengths):
    inputs = features[0]
    tok, width = inputs.shape
    n_seq = lax.axis_size("seq")
    n_batch = lax.axis_size("batch")
    total = tok * n_seq
    dim = width // HEADS
    scale = dim ** (-0.5)
    blocks = total // BLK
    chips = n_seq // 2
    half = tok // 2
    s = lax.axis_index("seq")
    core = s % 2

    def shift(x, by):
        return lax.ppermute(x, "seq", [(a, (a + 2 * by) % n_seq) for a in range(n_seq)])

    def swap(x):
        return lax.ppermute(x, "seq", [(a, a ^ 1) for a in range(n_seq)])

    def place(feats, mine, theirs, by):
        ordered = [jnp.where(core == 0, a, b) for a, b in zip(mine + theirs, theirs + mine)]
        first = (s // 2 + by) % chips * (2 * tok)
        return lax.dynamic_update_slice(feats, jnp.concatenate(ordered, axis=0), (first, 0))

    smem = pl.BlockSpec(memory_space=pltpu.SMEM)
    vmem = pl.BlockSpec(memory_space=pltpu.VMEM)
    hbm = pl.BlockSpec(memory_space=pltpu.HBM)
    params = pltpu.CompilerParams(vmem_limit_bytes=VMEM_LIMIT)

    plan, weights, feats = pl.pallas_call(
        functools.partial(prepare_kernel, blocks=blocks),
        in_specs=[smem] + [hbm] * 4,
        out_specs=[smem, vmem, hbm],
        out_shape=[
            jax.ShapeDtypeStruct((TABLE + blocks * blocks + UNROLL,), jnp.int32),
            jax.ShapeDtypeStruct((width, 4 * dim), BF16),
            jax.ShapeDtypeStruct((total, width), BF16),
        ],
        scratch_shapes=[pltpu.SemaphoreType.DMA((4,)), pltpu.SemaphoreType.DMA],
        compiler_params=params,
        cost_estimate=pl.CostEstimate(flops=0, bytes_accessed=8 * 10 ** 6, transcendentals=0),
        name="prepare",
    )(lengths, inputs, w_qk, w_value, w_gate)

    cots = jnp.moveaxis(cotangent[0].reshape(tok, HEADS, dim), 1, 0)
    cots = jnp.concatenate([cots, cots], axis=0)
    feats = lax.dynamic_update_slice(feats, swap(inputs), ((s - core + 1 - core) * tok, 0))
    right = left = inputs
    for step in range(1, chips // 2 + 1):
        last = step == chips // 2
        right = shift(right[:half] if last else right, 1)
        if step > 1:
            left, feats = lax.optimization_barrier((left, feats))
        left = shift(left[half:] if last else left, -1)
        if step == 2:
            cots, right, left = lax.optimization_barrier((cots, right, left))
        if step > 1:
            for piece in pending:
                feats = place(feats, *piece)
        if last:
            right, left, feats = lax.optimization_barrier((right, left, feats))
            feats = place(feats, (right, left), (swap(right), swap(left)), step)
        else:
            pending = [((right,), (swap(right),), -step), ((left,), (swap(left),), step)]
    cot = lax.all_to_all(cots, "seq", 0, 0).reshape(total, dim)

    row = jax.ShapeDtypeStruct((total, dim), BF16)
    rowf = jax.ShapeDtypeStruct((total, dim), F32)
    colf = jax.ShapeDtypeStruct((dim, total), F32)
    stat = jax.ShapeDtypeStruct((4, total), F32)
    q, k, v, pre, g, att, stats = pl.pallas_call(
        functools.partial(forward_kernel, scale=scale),
        in_specs=[smem, vmem, vmem, hbm],
        out_specs=[vmem] * 7,
        out_shape=[row, row, row, rowf, colf, colf, stat],
        scratch_shapes=[
            pltpu.VMEM((total, width), BF16),
            pltpu.VMEM((total, dim), F32),
            pltpu.SemaphoreType.DMA((total // WIDE,)),
        ],
        compiler_params=params,
        cost_estimate=pl.CostEstimate(flops=12 * 10 ** 9, bytes_accessed=12 * 10 ** 6, transcendentals=0),
        name="forward",
    )(plan, weights, cot, feats)

    count = dim
    which = lax.broadcasted_iota(jnp.int32, (4, 1), 0)
    for step in (1, 2, 4):
        other = lax.ppermute(stats, "seq", [(a, a ^ step) for a in range(n_seq)])
        both = stats + other
        delta = stats[0:1] - other[0:1]
        cross = jnp.where(which == 1, delta * (0.5 * count), 0.5 * (stats[2:3] - other[2:3]))
        stats = jnp.where(which == 0, 0.5 * both, jnp.where(which == 2, both, both + delta * cross))
        count = 2 * count

    part = pl.pallas_call(
        functools.partial(backward_kernel, scale=scale, width=width),
        in_specs=[smem, hbm] + [vmem] * 7,
        out_specs=vmem,
        out_shape=jax.ShapeDtypeStruct((dim, width), BF16),
        scratch_shapes=[
            pltpu.VMEM((total, width), BF16),
            pltpu.VMEM((total, dim), BF16),
            pltpu.VMEM((total, dim), F32),
            pltpu.VMEM((dim, total), BF16),
            pltpu.SemaphoreType.DMA,
        ],
        compiler_params=params,
        name="backward",
    )(plan, feats, q, k, v, pre, g, att, stats)
    parts = lax.all_to_all(part.reshape(n_batch, dim // n_batch, width), "batch", 0, 0)
    return jnp.sum(parts.astype(F32), axis=0)


def solution(mesh):
    return jax.shard_map(
        body,
        mesh=mesh,
        in_specs=(
            P("batch", "seq", None),
            P(),
            P(),
            P(),
            P("batch", "seq", None),
            P("batch", None),
        ),
        out_specs=P(("seq", "batch"), None),
        check_vma=False,
    )
```

```python
import functools
import jax
import jax.numpy as jnp
from jax import lax
from jax.experimental import pallas as pl
from jax.experimental.pallas import tpu as pltpu
from jax.sharding import PartitionSpec as P

HEADS = 8
BLK = 256
UNROLL = 4
WIDE = 512
F32 = jnp.float32
BF16 = jnp.bfloat16
ROLE, SECOND, THIRD, PLAIN, ALL, CHIP, CORE, TABLE = range(8)
VMEM_LIMIT = 46 * 1024 * 1024


def nn(a, b):
    return lax.dot_general(a, b, (((1,), (0,)), ((), ())), preferred_element_type=F32)


def nt(a, b):
    return lax.dot_general(a, b, (((1,), (1,)), ((), ())), preferred_element_type=F32)


def silu(z):
    half = 0.5 * z
    return half + half * jnp.tanh(half)


def silu_grad(z):
    half = 0.5 * z
    t = jnp.tanh(half)
    return 0.5 * (1.0 + t) * (1.0 + half * (1.0 - t))


def begin_of(pos, second, third):
    return jnp.where(pos >= third, third, jnp.where(pos >= second, second, 0))


def write_plan(plan, lengths, blocks):
    s = lax.axis_index("seq")
    second = lengths[0, 0]
    third = second + lengths[0, 1]
    plan[ROLE] = lax.div(s, HEADS)
    plan[SECOND] = second
    plan[THIRD] = third
    plan[CHIP] = lax.div(s, 2)
    plan[CORE] = lax.rem(s, 2)

    def emit(i, low, high, n):
        def put(j, at):
            plan[TABLE + at] = i * blocks + j
            return at + 1
        return lax.fori_loop(low, high, put, n)

    ranges = []
    for i in range(blocks):
        low = lax.div(begin_of(i * BLK, second, third), BLK)
        clear = lax.div(begin_of(i * BLK + BLK - 1, second, third) + BLK - 1, BLK)
        ranges.append((low, jnp.minimum(jnp.maximum(clear, low), i)))
    n = jnp.int32(0)
    for i, (low, clear) in enumerate(ranges):
        n = emit(i, clear, i, n)
    plan[PLAIN] = n
    for i, (low, clear) in enumerate(ranges):
        n = emit(i, low, clear, n)
        plan[TABLE + n] = i * blocks + i
        n = n + 1
    plan[ALL] = n
    for pad in range(UNROLL):
        plan[TABLE + n + pad] = blocks - 1


def block(index):
    return pl.ds(pl.multiple_of(index * BLK, BLK), BLK)


def tile_mask(i, j, second, third, query_rows):
    q_dim, shape = (0, (BLK, 128)) if query_rows else (1, (1, BLK))
    query = i * BLK + lax.broadcasted_iota(jnp.int32, shape, q_dim)
    begin = begin_of(query, second, third)
    if query_rows:
        parts = []
        for at in range(0, BLK, 128):
            key = j * BLK + at + lax.broadcasted_iota(jnp.int32, (BLK, 128), 1)
            parts.append((key <= query) & (key >= begin))
        return parts
    key = j * BLK + lax.broadcasted_iota(jnp.int32, (BLK, BLK), 0)
    return (key <= query) & (key >= begin)


def keep(values, mask):
    if isinstance(mask, list):
        cols = [jnp.where(m, values[:, n * 128:(n + 1) * 128], 0.0) for n, m in enumerate(mask)]
        return jnp.concatenate(cols, axis=1)
    return jnp.where(mask, values, 0.0)


def run_tiles(table, n_plain, n_all, blocks, begin_tile, end_tile):
    def entry(t):
        code = table[TABLE + t]
        i = code // blocks
        return i, code - i * blocks

    def group(masked):
        def f(u, carry):
            tiles = [entry(u * UNROLL + n) for n in range(UNROLL)]
            state = begin_tile(*tiles[0])
            for n, tile in enumerate(tiles):
                following = begin_tile(*tiles[n + 1]) if n + 1 < UNROLL else None
                end_tile(*tile, state, masked)
                state = following
            return carry
        return f

    plain = n_plain // UNROLL
    lax.fori_loop(0, plain, group(False), 0)
    lax.fori_loop(plain, (n_all + UNROLL - 1) // UNROLL, group(True), 0)


def prepare_kernel(lengths, own, wqk_hbm, wv_hbm, wu_hbm, plan, w_ref, feats, sem, own_sem, *, blocks):
    s = lax.axis_index("seq")
    dim = w_ref.shape[1] // 4
    head = lax.rem(s, HEADS) * dim
    width = wv_hbm.shape[1]
    tok = own.shape[0]
    copies = [pltpu.make_async_copy(own, feats.at[pl.ds(pl.multiple_of(s * tok, 16), tok), :], own_sem)]
    for n, (source, at) in enumerate(((wqk_hbm, head), (wqk_hbm, width + head), (wv_hbm, head), (wu_hbm, head))):
        columns = pl.ds(pl.multiple_of(at, 128), dim)
        copies.append(pltpu.make_async_copy(
            source.at[:, columns], w_ref.at[:, pl.ds(n * dim, dim)], sem.at[n]))
    for copy in copies:
        copy.start()
    write_plan(plan, lengths, blocks)
    for copy in copies:
        copy.wait()


def forward_kernel(plan, w_ref, cot, feats_hbm, q_ref, k_ref, v_ref, pre_ref, g_ref, att_ref,
                   stat_ref, feats, acc, sem, *, scale):
    role, second, third = plan[ROLE], plan[SECOND], plan[THIRD]
    total, dim = q_ref.shape
    blocks = total // BLK
    loads = []
    for i in range(total // WIDE):
        rows = pl.ds(i * WIDE, WIDE)
        loads.append(pltpu.make_async_copy(feats_hbm.at[rows, :], feats.at[rows, :], sem.at[i]))
        loads[-1].start()
    acc[...] = jnp.zeros_like(acc)
    for i in range(total // WIDE):
        rows = pl.ds(i * WIDE, WIDE)
        loads[i].wait()
        pre = nn(feats[rows, :], w_ref[...])
        pre_q, pre_k = pre[:, :dim], pre[:, dim:2 * dim]
        q_ref[rows, :] = silu(pre_q).astype(BF16)
        k_ref[rows, :] = silu(pre_k).astype(BF16)
        v_ref[rows, :] = silu(pre[:, 2 * dim:3 * dim]).astype(BF16)
        pre_ref[rows, :] = jnp.where(role == 0, pre_q, pre_k)
        g_ref[:, rows] = (cot[rows, :].astype(F32) * silu(pre[:, 3 * dim:])).T

    def begin_tile(i, j):
        return nt(q_ref[block(i), :], k_ref[block(j), :])

    def end_tile(i, j, scores, masked):
        half = scores * (0.5 * scale)
        w = half + half * jnp.tanh(half)
        if masked:
            w = keep(w, tile_mask(i, j, second, third, True))
        acc[block(i), :] += nn(w.astype(BF16), v_ref[block(j), :])

    run_tiles(plan, plan[PLAIN], plan[ALL], blocks, begin_tile, end_tile)
    for i in range(blocks):
        rows = pl.ds(i * BLK, BLK)
        att = acc[rows, :].T
        g = g_ref[:, rows]
        att_ref[:, rows] = att
        mean = jnp.mean(att, axis=0, keepdims=True)
        centered = att - mean
        stat_ref[0:1, rows] = mean
        stat_ref[1:2, rows] = jnp.sum(centered * centered, axis=0, keepdims=True)
        stat_ref[2:3, rows] = jnp.sum(g, axis=0, keepdims=True)
        stat_ref[3:4, rows] = jnp.sum(g * centered, axis=0, keepdims=True)


def backward_kernel(plan, feats_hbm, q_ref, k_ref, v_ref, pre_ref, g_ref, att_ref, stat_ref,
                    out_ref, feats, datt, acc, dpre, sem, *, scale, width):
    table = plan
    role, second, third = plan[ROLE], plan[SECOND], plan[THIRD]
    total = q_ref.shape[0]
    blocks = total // BLK
    load = pltpu.make_async_copy(feats_hbm, feats, sem)
    load.start()
    for i in range(blocks):
        rows = pl.ds(i * BLK, BLK)
        mean = stat_ref[0:1, rows]
        rstd = lax.rsqrt(stat_ref[1:2, rows] / width + 1e-5)
        g_mean = stat_ref[2:3, rows] / width
        gn_mean = stat_ref[3:4, rows] * rstd / width
        normed = (att_ref[:, rows] - mean) * rstd
        d = rstd * (g_ref[:, rows] - g_mean - normed * gn_mean)
        datt[rows, :] = d.T.astype(BF16)
    acc[...] = jnp.zeros_like(acc)

    def d_scores(scores, dw, mask):
        half = scores * (0.5 * scale)
        t = jnp.tanh(half)
        ds = ((0.5 * scale) + (0.5 * scale) * t) * (1.0 + half * (1.0 - t)) * dw
        if mask is not None:
            ds = keep(ds, mask)
        return ds.astype(BF16)

    def query_begin(i, j):
        return (nt(q_ref[block(i), :], k_ref[block(j), :]), nt(datt[block(i), :], v_ref[block(j), :]))

    def query_end(i, j, state, masked):
        ds = d_scores(*state, tile_mask(i, j, second, third, True) if masked else None)
        acc[block(i), :] += nn(ds, k_ref[block(j), :])

    def key_begin(i, j):
        return (nt(k_ref[block(j), :], q_ref[block(i), :]), nt(v_ref[block(j), :], datt[block(i), :]))

    def key_end(i, j, state, masked):
        ds = d_scores(*state, tile_mask(i, j, second, third, False) if masked else None)
        acc[block(j), :] += nn(ds, q_ref[block(i), :])

    pl.when(role == 0)(lambda: run_tiles(table, plan[PLAIN], plan[ALL], blocks, query_begin, query_end))
    pl.when(role == 1)(lambda: run_tiles(table, plan[PLAIN], plan[ALL], blocks, key_begin, key_end))
    for i in range(blocks):
        rows = pl.ds(i * BLK, BLK)
        dpre[:, rows] = (acc[rows, :] * silu_grad(pre_ref[rows, :])).T.astype(BF16)
    load.wait()
    out_ref[...] = nn(dpre[...], feats[...]).astype(out_ref.dtype)


def body(features, w_qk, w_value, w_gate, cotangent, lengths):
    inputs = features[0]
    tok, width = inputs.shape
    n_seq = lax.axis_size("seq")
    n_batch = lax.axis_size("batch")
    total = tok * n_seq
    dim = width // HEADS
    scale = dim ** (-0.5)
    blocks = total // BLK
    chips = n_seq // 2
    half = tok // 2
    s = lax.axis_index("seq")
    core = s % 2

    def shift(x, by):
        return lax.ppermute(x, "seq", [(a, (a + 2 * by) % n_seq) for a in range(n_seq)])

    def swap(x):
        return lax.ppermute(x, "seq", [(a, a ^ 1) for a in range(n_seq)])

    def place(feats, mine, theirs, by):
        ordered = [jnp.where(core == 0, a, b) for a, b in zip(mine + theirs, theirs + mine)]
        first = (s // 2 + by) % chips * (2 * tok)
        return lax.dynamic_update_slice(feats, jnp.concatenate(ordered, axis=0), (first, 0))

    smem = pl.BlockSpec(memory_space=pltpu.SMEM)
    vmem = pl.BlockSpec(memory_space=pltpu.VMEM)
    hbm = pl.BlockSpec(memory_space=pltpu.HBM)
    params = pltpu.CompilerParams(vmem_limit_bytes=VMEM_LIMIT)

    plan, weights, feats = pl.pallas_call(
        functools.partial(prepare_kernel, blocks=blocks),
        in_specs=[smem] + [hbm] * 4,
        out_specs=[smem, vmem, hbm],
        out_shape=[
            jax.ShapeDtypeStruct((TABLE + blocks * blocks + UNROLL,), jnp.int32),
            jax.ShapeDtypeStruct((width, 4 * dim), BF16),
            jax.ShapeDtypeStruct((total, width), BF16),
        ],
        scratch_shapes=[pltpu.SemaphoreType.DMA((4,)), pltpu.SemaphoreType.DMA],
        compiler_params=params,
        cost_estimate=pl.CostEstimate(flops=0, bytes_accessed=8 * 10 ** 6, transcendentals=0),
        name="prepare",
    )(lengths, inputs, w_qk, w_value, w_gate)

    cots = jnp.moveaxis(cotangent[0].reshape(tok, HEADS, dim), 1, 0)
    cots = jnp.concatenate([cots, cots], axis=0)
    feats = lax.dynamic_update_slice(feats, swap(inputs), ((s - core + 1 - core) * tok, 0))
    right = left = inputs
    for step in range(1, chips // 2 + 1):
        last = step == chips // 2
        if step > 2:
            right, left, feats = lax.optimization_barrier((right, left, feats))
        right = shift(right[:half] if last else right, 1)
        if step == 2:
            left, feats = lax.optimization_barrier((left, feats))
        left = shift(left[half:] if last else left, -1)
        if step == 2:
            cots, right, left = lax.optimization_barrier((cots, right, left))
        if step > 1:
            for piece in pending:
                feats = place(feats, *piece)
        if last:
            right, left, feats = lax.optimization_barrier((right, left, feats))
            feats = place(feats, (right, left), (swap(right), swap(left)), step)
        else:
            pending = [((right,), (swap(right),), -step), ((left,), (swap(left),), step)]
    cot = lax.all_to_all(cots, "seq", 0, 0).reshape(total, dim)

    row = jax.ShapeDtypeStruct((total, dim), BF16)
    rowf = jax.ShapeDtypeStruct((total, dim), F32)
    colf = jax.ShapeDtypeStruct((dim, total), F32)
    stat = jax.ShapeDtypeStruct((4, total), F32)
    q, k, v, pre, g, att, stats = pl.pallas_call(
        functools.partial(forward_kernel, scale=scale),
        in_specs=[smem, vmem, vmem, hbm],
        out_specs=[vmem] * 7,
        out_shape=[row, row, row, rowf, colf, colf, stat],
        scratch_shapes=[
            pltpu.VMEM((total, width), BF16),
            pltpu.VMEM((total, dim), F32),
            pltpu.SemaphoreType.DMA((total // WIDE,)),
        ],
        compiler_params=params,
        cost_estimate=pl.CostEstimate(flops=12 * 10 ** 9, bytes_accessed=12 * 10 ** 6, transcendentals=0),
        name="forward",
    )(plan, weights, cot, feats)

    count = dim
    which = lax.broadcasted_iota(jnp.int32, (4, 1), 0)
    for step in (1, 2, 4):
        other = lax.ppermute(stats, "seq", [(a, a ^ step) for a in range(n_seq)])
        both = stats + other
        delta = stats[0:1] - other[0:1]
        cross = jnp.where(which == 1, delta * (0.5 * count), 0.5 * (stats[2:3] - other[2:3]))
        stats = jnp.where(which == 0, 0.5 * both, jnp.where(which == 2, both, both + delta * cross))
        count = 2 * count

    part = pl.pallas_call(
        functools.partial(backward_kernel, scale=scale, width=width),
        in_specs=[smem, hbm] + [vmem] * 7,
        out_specs=vmem,
        out_shape=jax.ShapeDtypeStruct((dim, width), BF16),
        scratch_shapes=[
            pltpu.VMEM((total, width), BF16),
            pltpu.VMEM((total, dim), BF16),
            pltpu.VMEM((total, dim), F32),
            pltpu.VMEM((dim, total), BF16),
            pltpu.SemaphoreType.DMA,
        ],
        compiler_params=params,
        name="backward",
    )(plan, feats, q, k, v, pre, g, att, stats)
    parts = lax.all_to_all(part.reshape(n_batch, dim // n_batch, width), "batch", 0, 0)
    return jnp.sum(parts.astype(F32), axis=0)


def solution(mesh):
    return jax.shard_map(
        body,
        mesh=mesh,
        in_specs=(
            P("batch", "seq", None),
            P(),
            P(),
            P(),
            P("batch", "seq", None),
            P("batch", None),
        ),
        out_specs=P(("seq", "batch"), None),
        check_vma=False,
    )
```
